32 devices in a mesh: parts: 2 (over y), wide: 4 (over z), col: 2 (over x), pair: 2 (over core).
Axes of the slice: x: 2, y: 2, z: 4, core: 2. Of those that a mesh axis runs over, the one named last changes fastest.
Arguments:
- peram: bfloat16 [32, 384, 2, 384], P(('parts', 'wide'), ('col', 'pair')), parts along dimension 0, may hold values from -0.21875 to 0.21875
- elements: bfloat16 [8, 384, 2, 384], P('parts'), parts along dimension 0, may hold values from -6 to 6
- l1_peram: int32 [8, 4], P(('parts', 'wide')), parts along dimension 0, may hold values from 0 to 3
- l1_elem: int32 [8, 4], P(('parts', 'wide')), parts along dimension 0, may hold values from 0 to 3
- owners: int32 [8, 4], P(('parts', 'wide')), parts along dimension 0, may hold values from 0 to 1, as said below
- first_ops: int32 [8, 2, 4], P('parts', 'col'), parts along dimension 0, may hold values from 0 to 11, as said below
- second_ops: int32 [8, 2, 4], P(('parts', 'wide'), 'col'), parts along dimension 0, may hold values from 0 to 2, as said below
- product_ops: int32 [8, 2, 4, 2], P(('parts', 'wide'), 'col'), parts along dimension 0, may hold values from 0 to 3
- weights: int32 [16, 32], P('parts', ('wide', 'col')), parts along dimension 0, may hold values from -3 to 3
Outputs:
- products: bfloat16 [64, 2, 2, 96, 2, 384], P(('parts', 'wide', 'col'), None, 'pair'), parts along dimension 0
- diagrams: float32 [16, 2], P('parts'), parts along dimension 0
The draws below stay inside these ranges and needn't reach their ends.
There are 2 independent parts, one for each index of `parts`. The reference program is written for one: setup_inputs(seed, part) draws one part's arguments, and reference() takes and returns one part's arrays. A program takes and returns all parts, laid end to end along the dimension named above; each array names one. Nothing has to cross between parts.
Inputs may be any that keep to these rules, and one draw needn't show every extreme that they name: `owners`: in every wide group each col index owns 1 to 3 blocks, and some col index owns exactly 3. `first_ops`: for owner (g, c) an entry s * 3 + k names the k-th block of group s owned by col index c, k below the number of such blocks. At most 2 tasks of one owner name one group s, exactly 2 for some s of every owner, and tasks of one owner that name the same group name the same block. `second_ops`: entries of owner (g, c) are below the number of blocks of group g owned by col index c.
All inputs are finite; a program needn't handle non-finite values.
Results may differ from the reference program's by a relative error of at most 0.0082.
Values may be sent and summed in bfloat16 or wider, within the bound.
A program may use at most 128 MiB of HBM per device.

```python
import math
import jax
import jax.numpy as jnp
from jax import lax

NVEC = 384
NELEM = 4
PERAMS = 4
CAP_LANE = 3
PRODUCTS = 4
DIAGRAMS = 8
BLOCKS = 4
TASKS = 4
PERAMS_ALL = 16
PRODUCTS_ALL = 32
N_WIDE = 4
N_COL = 2
N_PAIR = 2


def lane_table(key):
    own_key = jax.random.fold_in(key, 101)

    def one_group(group_key):
        heavy_key, extra_key, order_key = jax.random.split(group_key, 3)
        heavy = jax.random.randint(heavy_key, (), 0, N_COL).astype(jnp.int32)
        spare = BLOCKS - N_COL - (CAP_LANE - 1)
        extra_slots = jax.random.permutation(extra_key, (N_COL - 1) * (CAP_LANE - 1))[:spare].astype(jnp.int32)
        other_lane = extra_slots // (CAP_LANE - 1)
        other_lane = other_lane + (other_lane >= heavy).astype(jnp.int32)
        lanes = jnp.concatenate([jnp.arange(N_COL, dtype=jnp.int32), jnp.full((CAP_LANE - 1,), heavy, jnp.int32), other_lane])
        return lanes[jax.random.permutation(order_key, BLOCKS)]
    owners = jax.vmap(one_group)(jax.random.split(own_key, N_WIDE))
    counts = jnp.sum((owners[:, :, None] == jnp.arange(N_COL, dtype=jnp.int32)[None, None, :]).astype(jnp.int32), axis=1)
    return (owners, counts)


def draw_owners(key, part):
    owners, counts = lane_table(key)
    return owners


def draw_first_ops(key, part):
    owners, counts = lane_table(key)
    key = jax.random.fold_in(key, 3)

    def one_owner(owner_key, lane):
        heavy_key, spread_key, rank_key, order_key = jax.random.split(owner_key, 4)
        heavy = jax.random.randint(heavy_key, (), 0, N_WIDE).astype(jnp.int32)
        others = jax.random.permutation(spread_key, N_WIDE - 1)[:N_WIDE - 2].astype(jnp.int32)
        others = others + (others >= heavy).astype(jnp.int32)
        sources = jnp.concatenate([jnp.full((2,), heavy, jnp.int32), others])
        lane_counts = counts[:, lane]
        ranks = jax.random.randint(rank_key, (N_WIDE,), 0, lane_counts).astype(jnp.int32)
        chosen = sources * CAP_LANE + ranks[sources]
        return chosen[jax.random.permutation(order_key, TASKS)]
    lanes_flat = jnp.tile(jnp.arange(N_COL, dtype=jnp.int32), N_WIDE)
    result = jax.vmap(one_owner)(jax.random.split(key, N_WIDE * N_COL), lanes_flat)
    return result.reshape(N_WIDE, N_COL, TASKS)


def draw_second_ops(key, part):
    owners, counts = lane_table(key)
    key = jax.random.fold_in(key, 5)
    return jax.random.randint(key, (N_WIDE, N_COL, TASKS), 0, counts[:, :, None]).astype(jnp.int32)


def plant(values, stream_key, least, high):
    shape = values.shape
    place = [jax.random.randint(jax.random.fold_in(stream_key, axis), (), 0, shape[axis]) for axis in range(len(shape))]
    values = values.at[tuple(place)].set(least)
    longest = shape.index(max(shape))
    place[longest] = (place[longest] + 1) % shape[longest]
    return values.at[tuple(place)].set(high)


def levels(rng, dims, cuts, low, high):
    def one(axis_at, blocks):
        steps = jax.random.uniform(jax.random.fold_in(jax.random.fold_in(rng, 6), axis_at), (blocks,), jnp.float32, low / len(cuts), high / len(cuts))
        return jnp.repeat(jnp.exp(steps), dims[axis_at] // blocks).reshape((-1,) + (1,) * (len(dims) - axis_at - 1))

    factor_of = one(*cuts[0])
    for cut in cuts[1:]:
        factor_of = factor_of * one(*cut)
    return factor_of


def centred(stream_key, extent, spread, limit, shards=(), kind=jnp.bfloat16):
    level = levels(stream_key, extent, shards, -0.22, 0.18) if shards else 1.0
    drawn = jax.random.normal(stream_key, extent, jnp.float32) * spread * level
    return jnp.minimum(jnp.maximum(drawn, -limit), limit).astype(kind)


def setup_inputs(seed: int = 0, part: int = 0) -> dict:
    keys = jax.random.split(jax.random.key(seed), 10)
    own_keys = jax.random.split(jax.random.fold_in(keys[9], part), 10)
    return {
        "peram": centred(own_keys[0], (PERAMS_ALL, NVEC, 2, NVEC), (2 * NVEC) ** -0.5, 0.21875, ((0, 4), (1, 4))),
        "elements": centred(own_keys[1], (NELEM, NVEC, 2, NVEC), 1.0, 6.0),
        "l1_peram": plant(jax.random.randint(own_keys[2], (N_WIDE, BLOCKS), 0, PERAMS), jax.random.fold_in(own_keys[2], 1), 0, PERAMS - 1).astype(jnp.int32),
        "l1_elem": plant(jax.random.randint(own_keys[3], (N_WIDE, BLOCKS), 0, NELEM), jax.random.fold_in(own_keys[3], 1), 0, NELEM - 1).astype(jnp.int32),
        "owners": draw_owners(jax.random.fold_in(jax.random.fold_in(keys[9], part), 71), part),
        "first_ops": draw_first_ops(jax.random.fold_in(jax.random.fold_in(keys[9], part), 71), part),
        "second_ops": draw_second_ops(jax.random.fold_in(jax.random.fold_in(keys[9], part), 71), part),
        "product_ops": plant(jax.random.randint(own_keys[7], (N_WIDE, N_COL, PRODUCTS, 2), 0, TASKS), jax.random.fold_in(own_keys[7], 1), 0, TASKS - 1).astype(jnp.int32),
        "weights": plant(jax.random.randint(own_keys[8], (DIAGRAMS, PRODUCTS_ALL), -3, 4), jax.random.fold_in(own_keys[8], 1), -3, 3).astype(jnp.int32),
    }


def complex_mul(left, right, factor):
    left_real = left[..., 0, :]
    left_imag = left[..., 1, :]
    right_real = right[..., 0, :]
    right_imag = right[..., 1, :]
    high = lax.Precision.HIGHEST
    real_part = jnp.einsum('...rk,...kj->...rj', left_real, right_real, precision=high) - jnp.einsum('...rk,...kj->...rj', left_imag, right_imag, precision=high)
    imag_part = jnp.einsum('...rk,...kj->...rj', left_real, right_imag, precision=high) + jnp.einsum('...rk,...kj->...rj', left_imag, right_real, precision=high)
    return jnp.stack([real_part, imag_part], axis=-2) * factor

def reference(peram, elements, l1_peram, l1_elem, owners, first_ops, second_ops, product_ops, weights):
    factor = 1.0 / math.sqrt(2.0 * NVEC)
    group_ids = jnp.arange(N_WIDE, dtype=jnp.int32)[:, None]
    peram_ids = (group_ids * PERAMS + l1_peram).reshape(-1).astype(jnp.int32)
    elem_ids = l1_elem.reshape(-1).astype(jnp.int32)

    def level_one(ids):
        peram_id, elem_id = ids
        return complex_mul(peram[peram_id].astype(jnp.float32), elements[elem_id].astype(jnp.float32), 1.0).astype(jnp.bfloat16)
    blocks = lax.map(level_one, (peram_ids, elem_ids))
    per_group = owners.shape[1]
    lane_hot = (owners[:, :, None] == jnp.arange(N_COL, dtype=jnp.int32)[None, None, :]).astype(jnp.int32)
    lane_rank = lax.optimization_barrier(jnp.sum((jnp.cumsum(lane_hot, axis=1) - lane_hot) * lane_hot, axis=2))
    rank_hot = (lane_rank[:, :, None] == jnp.arange(CAP_LANE, dtype=jnp.int32)[None, None, :]).astype(jnp.int32)
    block_ids = jnp.arange(per_group, dtype=jnp.int32)[None, :, None, None]
    table = lax.optimization_barrier(jnp.sum(block_ids * lane_hot[:, :, :, None] * rank_hot[:, :, None, :], axis=1)).astype(jnp.int32)

    def per_owner(owner_id):
        group = owner_id // N_COL
        lane = owner_id % N_COL
        first_row = first_ops[group, lane]
        second_row = second_ops[group, lane]
        pairs_row = product_ops[group, lane]
        sources = (first_row // CAP_LANE).astype(jnp.int32)
        ranks = (first_row % CAP_LANE).astype(jnp.int32)
        left_ids = sources * per_group + table[sources, lane, ranks]
        right_ids = group * per_group + table[group, lane, second_row]
        level_two = complex_mul(blocks[left_ids].astype(jnp.float32), blocks[right_ids].astype(jnp.float32), factor).astype(jnp.bfloat16)
        full = complex_mul(level_two[pairs_row[:, 0]].astype(jnp.float32), level_two[pairs_row[:, 1]].astype(jnp.float32), factor)
        traces = jnp.trace(full, axis1=1, axis2=3)
        return (full.astype(jnp.bfloat16), traces)
    owner_ids = jnp.arange(N_WIDE * N_COL, dtype=jnp.int32)
    products, traces = lax.map(per_owner, owner_ids)
    products = products.reshape(N_WIDE * N_COL * PRODUCTS, N_COL, N_PAIR, NVEC // (N_COL * N_PAIR), 2, NVEC)
    traces = traces.reshape(N_WIDE * N_COL * PRODUCTS, 2)
    diagrams = jnp.dot(weights.astype(jnp.float32), traces, precision=lax.Precision.HIGHEST) / NVEC
    return (products, diagrams)
```

```python
import math

import jax
import jax.numpy as jnp
from jax import lax
from jax.experimental import pallas as pl
from jax.experimental.pallas import tpu as pltpu
from jax.sharding import PartitionSpec as P

CAP_LANE = 3
MESH = pl.DeviceIdType.MESH


def contract(
    lanes,
    peers,
    perams_ref,
    elems_ref,
    weights_ref,
    l1_peram,
    l1_elem,
    owners,
    first_ops,
    second_ops,
    product_ops,
    out_ref,
    diag_ref,
    big_elem,
    x_stage,
    own,
    arrived,
    paired,
    z_stage,
    pool,
    big_right,
    q_own,
    q_other,
    big_q,
    mask,
    term,
    terms,
    x_send,
    x_recv,
    p_send,
    p_recv,
    z_send,
    z_recv,
    q_send,
    q_recv,
    d_send,
    d_recv,
):
    here = lax.axis_index("wide")
    lane = lax.axis_index("col")
    half = lax.axis_index("pair")
    nelem, nvec, wide2 = elems_ref.shape
    rows = perams_ref.shape[1]
    half_rows = lanes * rows
    nblocks = owners.shape[1]
    tasks = second_ops.shape[2]
    nproducts = product_ops.shape[2]
    factor = 1.0 / math.sqrt(2.0 * nvec)
    total = peers * lanes * 2
    mine = (here * lanes + lane) * 2 + half

    def coords(index):
        return {"wide": index // (lanes * 2), "col": index // 2 % lanes, "pair": index % 2}

    barrier = pltpu.get_barrier_semaphore()

    def greet(i, carry):
        other = lax.rem(mine + 1 + i, total)
        pl.semaphore_signal(barrier, inc=1, device_id=coords(other), device_id_type=MESH)
        return carry

    lax.fori_loop(0, total - 1, greet, 0)

    def flat(block):
        if rows % 16 == 0:
            return block.reshape(-1, wide2)
        return block.astype(jnp.float32).reshape(-1, wide2).astype(jnp.bfloat16)

    def split(block):
        return block.reshape(lanes, rows, wide2)

    def expand(target, y):
        target[:nvec, :] = y
        target[nvec:, :nvec] = -y[:, nvec:]
        target[nvec:, nvec:] = y[:, :nvec]

    for e in range(nelem):
        expand(big_elem.at[e], elems_ref[e])

    def blocks_of(which):
        found = [jnp.int32(0)] * CAP_LANE
        count = jnp.int32(0)
        for b in range(nblocks):
            match = (owners[0, b] == which).astype(jnp.int32)
            for k in range(CAP_LANE):
                found[k] = jnp.where((match == 1) & (count == k), jnp.int32(b), found[k])
            count = count + match
        return found

    def level_one(b):
        left = perams_ref[l1_peram[0, b]]
        return jnp.dot(
            left, big_elem[l1_elem[0, b]], preferred_element_type=jnp.float32
        ).astype(jnp.bfloat16)

    def x_copy(j, k):
        return pltpu.make_async_remote_copy(
            src_ref=x_stage.at[j, k],
            dst_ref=arrived.at[lane, k],
            send_sem=x_send.at[j, k],
            recv_sem=x_recv.at[j, k],
            device_id={"col": lax.rem(lane + 1 + j, lanes)},
            device_id_type=MESH,
        )

    def p_copy(j):
        q = lax.rem(lane + lanes - j, lanes)
        return pltpu.make_async_remote_copy(
            src_ref=own if j == 0 else arrived.at[q],
            dst_ref=paired.at[q],
            send_sem=p_send.at[j],
            recv_sem=p_recv.at[j],
            device_id={"pair": 1 - half},
            device_id_type=MESH,
        )

    def z_copy(i, j):
        q = lax.rem(lane + lanes - j, lanes)
        return pltpu.make_async_remote_copy(
            src_ref=z_stage.at[i, q],
            dst_ref=pool.at[here, q],
            send_sem=z_send.at[i, j],
            recv_sem=z_recv.at[i, j],
            device_id={"wide": lax.rem(here + 1 + i, peers)},
            device_id_type=MESH,
        )

    def q_copy(t):
        return pltpu.make_async_remote_copy(
            src_ref=q_own.at[t],
            dst_ref=q_other.at[t],
            send_sem=q_send.at[t],
            recv_sem=q_recv.at[t],
            device_id={"pair": 1 - half},
            device_id_type=MESH,
        )

    def d_copy(i):
        return pltpu.make_async_remote_copy(
            src_ref=term,
            dst_ref=terms.at[mine],
            send_sem=d_send.at[i],
            recv_sem=d_recv.at[i],
            device_id=coords(lax.rem(mine + 1 + i, total)),
            device_id_type=MESH,
        )

    def rank_for(group):
        chosen = jnp.int32(0)
        for t in range(tasks):
            entry = first_ops[group, 0, t]
            chosen = jnp.where(entry // CAP_LANE == here, entry % CAP_LANE, chosen)
        return chosen

    ready = False
    for j in range(lanes - 1):
        picked = blocks_of(lax.rem(lane + 1 + j, lanes))
        for k in range(CAP_LANE):
            x_stage[j, k] = level_one(picked[k])
            if not ready:
                pl.semaphore_wait(barrier, total - 1)
                ready = True
            x_copy(j, k).start()
    picked = blocks_of(lane)
    for k in range(CAP_LANE):
        block = level_one(picked[k])
        own[k] = block
        arrived[lane, k] = block
    ranks = [rank_for(lax.rem(here + 1 + i, peers)) for i in range(peers - 1)]
    rank_here = rank_for(here)
    for i in range(peers - 1):
        z_stage[i, lane] = own[ranks[i]]
        z_copy(i, 0).start()
    p_copy(0).start()
    pool[here, lane] = own[rank_here]

    row_ids = lax.broadcasted_iota(jnp.int32, (rows, nvec), 0)
    col_ids = lax.broadcasted_iota(jnp.int32, (rows, nvec), 1)
    for q in range(lanes):
        mask[q * rows : (q + 1) * rows, :] = (
            col_ids == row_ids + (2 * q + half) * rows
        ).astype(jnp.float32)

    for j in range(lanes - 1):
        for k in range(CAP_LANE):
            x_copy(j, k).wait_recv()
    for j in range(1, lanes):
        q = lax.rem(lane + lanes - j, lanes)
        for i in range(peers - 1):
            z_stage[i, q] = arrived[q, ranks[i]]
            z_copy(i, j).start()
        p_copy(j).start()
        pool[here, q] = arrived[q, rank_here]
    for j in range(lanes):
        p_copy(j).wait_recv()

    lower = (half == 0).astype(jnp.float32)

    def both_halves(target, mine_half, other_half):
        pieces = []
        for q in range(lanes):
            a = mine_half(q).astype(jnp.float32)
            b = other_half(q).astype(jnp.float32)
            pieces.append(jnp.where(lower > 0.5, a, b))
            pieces.append(jnp.where(lower > 0.5, b, a))
        expand(target, jnp.concatenate(pieces, axis=0).astype(jnp.bfloat16))

    for k in range(CAP_LANE):
        both_halves(big_right.at[k], lambda q: arrived[q, k], lambda q: paired[q, k])

    for j in range(lanes):
        for i in range(peers - 1):
            z_copy(i, j).wait_recv()

    def one_task(t, carry):
        left = flat(pool[first_ops[here, 0, t] // CAP_LANE])
        full = jnp.dot(left, big_right[second_ops[0, 0, t]], preferred_element_type=jnp.float32)
        q_own[t] = split(full * factor).astype(jnp.bfloat16)
        q_copy(t).start()
        return carry

    lax.fori_loop(0, tasks, one_task, 0)

    for j in range(lanes - 1):
        for k in range(CAP_LANE):
            x_copy(j, k).wait_send()
    for j in range(lanes):
        p_copy(j).wait_send()
        for i in range(peers - 1):
            z_copy(i, j).wait_send()

    def q_done(t, carry):
        q_copy(t).wait()
        return carry

    lax.fori_loop(0, tasks, q_done, 0)
    term[...] = jnp.zeros_like(term)

    for v in range(nproducts):
        left_id = product_ops[0, 0, v, 0]
        right_id = product_ops[0, 0, v, 1]
        both_halves(big_q, lambda q: q_own[right_id, q], lambda q: q_other[right_id, q])
        full = jnp.dot(flat(q_own[left_id]), big_q[...], preferred_element_type=jnp.float32) * factor
        out_ref[v] = split(full).astype(jnp.bfloat16)
        weight = weights_ref[:, v : v + 1].astype(jnp.float32)
        for part in range(2):
            picked_diag = jnp.sum(
                full[:, part * nvec : (part + 1) * nvec] * mask[...], axis=0, keepdims=True
            )
            folded = sum(picked_diag[:, n : n + 128] for n in range(0, nvec, 128))
            term[:, part * 128 : (part + 1) * 128] += weight * folded

    terms[mine] = term[...]

    def d_start(i, carry):
        d_copy(i).start()
        return carry

    def d_done(i, carry):
        d_copy(i).wait()
        return carry

    lax.fori_loop(0, total - 1, d_start, 0)
    lax.fori_loop(0, total - 1, d_done, 0)
    summed = lax.fori_loop(0, total, lambda i, acc: acc + terms[i], jnp.zeros_like(term))
    diag_ref[:, 0:1] = jnp.sum(summed[:, :128], axis=1, keepdims=True) / nvec
    diag_ref[:, 1:2] = jnp.sum(summed[:, 128:], axis=1, keepdims=True) / nvec


def shards(peram, elements, l1_peram, l1_elem, owners, first_ops, second_ops, product_ops, weights):
    nelem, nvec = elements.shape[:2]
    nperam, rows = peram.shape[:2]
    lanes = lax.axis_size("col")
    peers = lax.axis_size("wide")
    tasks = second_ops.shape[2]
    nproducts = product_ops.shape[2]
    diagrams = weights.shape[0]
    width = 2 * nvec
    total = peers * lanes * 2
    vmem = pl.BlockSpec(memory_space=pltpu.VMEM)
    smem = pl.BlockSpec(memory_space=pltpu.SMEM)
    bf16 = jnp.bfloat16

    def kernel(*refs):
        contract(lanes, peers, *refs)

    products, sums = pl.pallas_call(
        kernel,
        out_shape=(
            jax.ShapeDtypeStruct((nproducts, lanes, rows, width), bf16),
            jax.ShapeDtypeStruct((diagrams, 2), jnp.float32),
        ),
        in_specs=[vmem] * 3 + [smem] * 6,
        out_specs=(vmem, vmem),
        scratch_shapes=[
            pltpu.VMEM((nelem, width, width), bf16),
            pltpu.VMEM((max(lanes - 1, 1), CAP_LANE, rows, width), bf16),
            pltpu.VMEM((CAP_LANE, rows, width), bf16),
            pltpu.VMEM((lanes, CAP_LANE, rows, width), bf16),
            pltpu.VMEM((lanes, CAP_LANE, rows, width), bf16),
            pltpu.VMEM((peers, lanes, rows, width), bf16),
            pltpu.VMEM((peers, lanes, rows, width), bf16),
            pltpu.VMEM((CAP_LANE, width, width), bf16),
            pltpu.VMEM((tasks, lanes, rows, width), bf16),
            pltpu.VMEM((tasks, lanes, rows, width), bf16),
            pltpu.VMEM((width, width), bf16),
            pltpu.VMEM((lanes * rows, nvec), jnp.float32),
            pltpu.VMEM((diagrams, 256), jnp.float32),
            pltpu.VMEM((total, diagrams, 256), jnp.float32),
            pltpu.SemaphoreType.DMA((lanes, CAP_LANE)),
            pltpu.SemaphoreType.DMA((lanes, CAP_LANE)),
            pltpu.SemaphoreType.DMA((lanes,)),
            pltpu.SemaphoreType.DMA((lanes,)),
            pltpu.SemaphoreType.DMA((peers, lanes)),
            pltpu.SemaphoreType.DMA((peers, lanes)),
            pltpu.SemaphoreType.DMA((tasks,)),
            pltpu.SemaphoreType.DMA((tasks,)),
            pltpu.SemaphoreType.DMA((total,)),
            pltpu.SemaphoreType.DMA((total,)),
        ],
        compiler_params=pltpu.CompilerParams(
            collective_id=0, has_side_effects=True, vmem_limit_bytes=58 * 2**20
        ),
    )(
        peram.reshape(nperam, rows, width),
        elements.reshape(nelem, nvec, width),
        weights,
        l1_peram,
        l1_elem,
        owners,
        first_ops,
        second_ops,
        product_ops,
    )
    return (products.reshape(nproducts, lanes, 1, rows, 2, nvec), sums)


def solution(mesh):
    placed = (
        P(("parts", "wide"), ("col", "pair"), None, None),
        P("parts", None, None, None),
        P(("parts", "wide"), None),
        P(("parts", "wide"), None),
        P(("parts", "wide"), None),
        P("parts", "col", None),
        P(("parts", "wide"), "col", None),
        P(("parts", "wide"), "col", None, None),
        P("parts", ("wide", "col")),
    )
    return jax.shard_map(
        shards,
        mesh=mesh,
        in_specs=placed,
        out_specs=(P(("parts", "wide", "col"), None, "pair", None, None, None), P("parts", None)),
        check_vma=False,
    )
```

```python
import math

import jax
import jax.numpy as jnp
from jax import lax
from jax.experimental import pallas as pl
from jax.experimental.pallas import tpu as pltpu
from jax.sharding import PartitionSpec as P

CAP_LANE = 3
MESH = pl.DeviceIdType.MESH


def contract(
    lanes,
    peers,
    perams_ref,
    elems_ref,
    weights_ref,
    l1_elem_vec,
    owners_vec,
    l1_peram,
    l1_elem,
    owners,
    first_ops,
    second_ops,
    product_ops,
    out_ref,
    diag_ref,
    elems_raw,
    big_elem,
    x_stage,
    own,
    arrived,
    paired,
    z_stage,
    pool,
    half_raw,
    full_raw,
    left_wide,
    right_wide,
    left_ops,
    big_right,
    q_own,
    q_other,
    big_q,
    mask,
    term,
    terms,
    ids_vec,
    ids,
    e_sem,
    ids_sem,
    x_send,
    x_recv,
    p_send,
    p_recv,
    z_send,
    z_recv,
    i_send,
    i_recv,
    q_send,
    q_recv,
    d_send,
    d_recv,
):
    here = lax.axis_index("wide")
    lane = lax.axis_index("col")
    half = lax.axis_index("pair")
    nelem = elems_ref.shape[0]
    nvec = left_wide.shape[1] // 2
    wide2 = 2 * nvec
    rows = perams_ref.shape[1]
    strips = nvec // 128
    half_rows = lanes * rows
    nblocks = owners.shape[1]
    tasks = second_ops.shape[2]
    nproducts = product_ops.shape[3]
    factor = 1.0 / math.sqrt(2.0 * nvec)
    total = peers * lanes * 2
    mine = (here * lanes + lane) * 2 + half
    bf16 = jnp.bfloat16

    def elem_copy(e):
        return pltpu.make_async_copy(elems_ref.at[e], elems_raw.at[e], e_sem.at[e])

    for e in range(nelem):
        elem_copy(e).start()

    def coords(index):
        return {"wide": index // (lanes * 2), "col": index // 2 % lanes, "pair": index % 2}

    barrier = pltpu.get_barrier_semaphore()

    def greet(i, carry):
        other = lax.rem(mine + 1 + i, total)
        pl.semaphore_signal(barrier, inc=1, device_id=coords(other), device_id_type=MESH)
        return carry

    lax.fori_loop(0, total - 1, greet, 0)

    def flat(block):
        if rows % 16 == 0:
            return block.reshape(-1, wide2)
        return block.astype(jnp.float32).reshape(-1, wide2).astype(bf16)

    def split(block):
        return block.reshape(lanes, rows, wide2)

    def expand(target, y):
        target[:nvec, :] = y
        target[nvec:, :nvec] = -y[:, nvec:]
        target[nvec:, nvec:] = y[:, :nvec]

    def strip(j, base=0):
        return slice(base + j * 128, base + (j + 1) * 128)

    def columns(raw, count):
        for j in range(strips):
            for c in range(2):
                yield c, j, raw[j, pl.ds(c, count, stride=2), :].astype(bf16)

    def gather_columns(target, raw):
        for c, j, block in columns(raw, target.shape[0]):
            target[:, strip(j, c * nvec)] = block

    def as_rows(block):
        return block.astype(jnp.float32).reshape(-1, 128)

    def blocks_of(which, owner_at):
        found = [jnp.int32(0)] * CAP_LANE
        count = jnp.int32(0)
        for b in range(nblocks):
            match = (owner_at(b) == which).astype(jnp.int32)
            for k in range(CAP_LANE):
                found[k] = jnp.where((match == 1) & (count == k), jnp.int32(b), found[k])
            count = count + match
        return found

    def x_copy(j, k):
        return pltpu.make_async_remote_copy(
            src_ref=x_stage.at[j, k],
            dst_ref=arrived.at[lane, k],
            send_sem=x_send.at[j, k],
            recv_sem=x_recv.at[j, k],
            device_id={"col": lax.rem(lane + 1 + j, lanes)},
            device_id_type=MESH,
        )

    def p_copy(j):
        q = lax.rem(lane + lanes - j, lanes)
        return pltpu.make_async_remote_copy(
            src_ref=own if j == 0 else arrived.at[q],
            dst_ref=paired.at[q],
            send_sem=p_send.at[j],
            recv_sem=p_recv.at[j],
            device_id={"pair": 1 - half},
            device_id_type=MESH,
        )

    def z_copy(i, j):
        q = lax.rem(lane + lanes - j, lanes)
        return pltpu.make_async_remote_copy(
            src_ref=z_stage.at[i, q],
            dst_ref=pool.at[here, q],
            send_sem=z_send.at[i, j],
            recv_sem=z_recv.at[i, j],
            device_id={"wide": lax.rem(here + 1 + i, peers)},
            device_id_type=MESH,
        )

    def i_copy(i):
        return pltpu.make_async_remote_copy(
            src_ref=ids_vec.at[here],
            dst_ref=ids_vec.at[here],
            send_sem=i_send.at[i],
            recv_sem=i_recv.at[i],
            device_id={"wide": lax.rem(here + 1 + i, peers)},
            device_id_type=MESH,
        )

    def q_copy(t):
        return pltpu.make_async_remote_copy(
            src_ref=q_own.at[t],
            dst_ref=q_other.at[t],
            send_sem=q_send.at[t],
            recv_sem=q_recv.at[t],
            device_id={"pair": 1 - half},
            device_id_type=MESH,
        )

    def d_copy(i):
        return pltpu.make_async_remote_copy(
            src_ref=term,
            dst_ref=terms.at[mine],
            send_sem=d_send.at[i],
            recv_sem=d_recv.at[i],
            device_id=coords(lax.rem(mine + 1 + i, total)),
            device_id_type=MESH,
        )

    def rank_for(group):
        chosen = jnp.int32(0)
        for t in range(tasks):
            entry = first_ops[group, 0, t]
            chosen = jnp.where(entry // CAP_LANE == here, entry % CAP_LANE, chosen)
        return chosen

    ids_vec[here] = jnp.zeros(ids_vec.shape[1:], jnp.int32)
    ids_vec[here, 0:1, 0:nblocks] = l1_elem_vec[...]
    ids_vec[here, 1:2, 0:nblocks] = owners_vec[...]
    ready = False
    for j in range(lanes - 1):
        picked = blocks_of(lax.rem(lane + 1 + j, lanes), lambda b: owners[0, b])
        for k in range(CAP_LANE):
            x_stage[j, k] = perams_ref[l1_peram[0, picked[k]]]
            if not ready:
                pl.semaphore_wait(barrier, total - 1)
                ready = True
            x_copy(j, k).start()
    for i in range(peers - 1):
        i_copy(i).start()
    picked = blocks_of(lane, lambda b: owners[0, b])
    for k in range(CAP_LANE):
        block = perams_ref[l1_peram[0, picked[k]]]
        own[k] = block
    ranks = [rank_for(lax.rem(here + 1 + i, peers)) for i in range(peers - 1)]
    rank_here = rank_for(here)
    for i in range(peers - 1):
        z_stage[i, lane] = own[ranks[i]]
        z_copy(i, 0).start()
    p_copy(0).start()
    pool[here, lane] = own[rank_here]

    row_ids = lax.broadcasted_iota(jnp.int32, (rows, nvec), 0)
    col_ids = lax.broadcasted_iota(jnp.int32, (rows, nvec), 1)
    for q in range(lanes):
        mask[q * rows : (q + 1) * rows, :] = (
            col_ids == row_ids + (2 * q + half) * rows
        ).astype(jnp.float32)

    def convert_elem(e):
        elem_copy(e).wait()
        for j in range(strips):
            full_raw[j] = as_rows(elems_raw[e, :, :, strip(j)])
        for c, j, block in columns(full_raw, nvec):
            low, high = j * 128, (j + 1) * 128
            if c == 0:
                big_elem[e, :nvec, low:high] = block
                big_elem[e, nvec:, nvec + low : nvec + high] = block
            else:
                big_elem[e, :nvec, nvec + low : nvec + high] = block
                big_elem[e, nvec:, low:high] = -block

    convert_elem(0)
    for j in range(lanes - 1):
        for k in range(CAP_LANE):
            x_copy(j, k).wait_recv()
    for j in range(1, lanes):
        q = lax.rem(lane + lanes - j, lanes)
        for i in range(peers - 1):
            z_stage[i, q] = arrived[q, ranks[i]]
            z_copy(i, j).start()
        p_copy(j).start()
        pool[here, q] = arrived[q, rank_here]
    for e in range(1, nelem):
        convert_elem(e)
    for i in range(peers - 1):
        i_copy(i).wait()
    ids_copy = pltpu.make_async_copy(ids_vec, ids, ids_sem)
    ids_copy.start()
    ids_copy.wait()
    for j in range(lanes):
        p_copy(j).wait_recv()

    for k in range(CAP_LANE):
        for n in range(lanes):
            q = lax.rem(lane + lanes - n, lanes)
            for side in range(2):
                at = half if side == 0 else 1 - half
                start = pl.multiple_of((2 * q + at) * (2 * rows), 8)
                for j in range(strips):
                    if side == 1:
                        block = paired[q, k, :, :, strip(j)]
                    elif n == 0:
                        block = own[k, :, :, strip(j)]
                    else:
                        block = arrived[q, k, :, :, strip(j)]
                    full_raw[j, pl.ds(start, 2 * rows), :] = as_rows(block)
        gather_columns(right_wide, full_raw)
        block = jnp.dot(
            right_wide[...],
            big_elem[l1_elem[0, picked[k]]],
            preferred_element_type=jnp.float32,
        )
        expand(big_right.at[k], block.astype(bf16))

    def source_element(source):
        wanted = jnp.int32(0)
        for t in range(tasks):
            entry = first_ops[here, 0, t]
            wanted = jnp.where(entry // CAP_LANE == source, entry % CAP_LANE, wanted)
        found = blocks_of(lane, lambda b: ids[source, 1, b])
        chosen = found[0]
        for k in range(1, CAP_LANE):
            chosen = jnp.where(wanted == k, found[k], chosen)
        return ids[source, 0, chosen]

    def make_left(source):
        for j in range(strips):
            half_raw[j] = as_rows(pool[source, :, :, :, strip(j)])
        gather_columns(left_wide, half_raw)
        left_ops[source] = jnp.dot(
            left_wide[...],
            big_elem[source_element(source)],
            preferred_element_type=jnp.float32,
        ).astype(bf16)

    make_left(here)

    def one_source(i, carry):
        for j in range(lanes):
            z_copy(i, j).wait_recv()
        make_left(lax.rem(here + peers - 1 - i, peers))
        return carry

    lax.fori_loop(0, peers - 1, one_source, 0)

    def one_task(t, carry):
        left = left_ops[first_ops[here, 0, t] // CAP_LANE]
        full = jnp.dot(left, big_right[second_ops[0, 0, t]], preferred_element_type=jnp.float32)
        q_own[t] = split(full * factor).astype(bf16)
        q_copy(t).start()
        return carry

    lax.fori_loop(0, tasks, one_task, 0)

    for j in range(lanes - 1):
        for k in range(CAP_LANE):
            x_copy(j, k).wait_send()
    for j in range(lanes):
        p_copy(j).wait_send()
        for i in range(peers - 1):
            z_copy(i, j).wait_send()

    def q_done(t, carry):
        q_copy(t).wait()
        return carry

    lax.fori_loop(0, tasks, q_done, 0)

    def both_halves(target, mine_half, other_half):
        pieces = []
        for q in range(lanes):
            a = mine_half(q).astype(jnp.float32)
            b = other_half(q).astype(jnp.float32)
            pieces.append(jnp.where(half == 0, a, b))
            pieces.append(jnp.where(half == 0, b, a))
        expand(target, jnp.concatenate(pieces, axis=0).astype(bf16))

    sums = [jnp.zeros((1, term.shape[1]), jnp.float32)] * 2
    for v in range(nproducts):
        left_id = product_ops[0, 0, 0, v]
        right_id = product_ops[0, 0, 1, v]
        both_halves(big_q, lambda q: q_own[right_id, q], lambda q: q_other[right_id, q])
        full = jnp.dot(flat(q_own[left_id]), big_q[...], preferred_element_type=jnp.float32) * factor
        weight = weights_ref[v : v + 1, :].astype(jnp.float32)
        for c in range(2):
            for j in range(strips):
                half_raw[j, pl.ds(c, half_rows, stride=2), :] = full[:, strip(j, c * nvec)]
            picked_diag = jnp.sum(
                full[:, c * nvec : (c + 1) * nvec] * mask[...], axis=0, keepdims=True
            )
            sums[c] = sums[c] + weight * jnp.sum(picked_diag, axis=1, keepdims=True)
        for j in range(strips):
            out_ref[v, :, 0, :, :, strip(j)] = (
                half_raw[j].astype(bf16).reshape(lanes, rows, 2, 128)
            )

    for c in range(2):
        term[c : c + 1, :] = sums[c]
    terms[mine] = term[...]

    def d_start(i, carry):
        d_copy(i).start()
        return carry

    def d_done(i, carry):
        d_copy(i).wait()
        return carry

    lax.fori_loop(0, total - 1, d_start, 0)
    lax.fori_loop(0, total - 1, d_done, 0)
    summed = lax.fori_loop(0, total, lambda i, acc: acc + terms[i], jnp.zeros_like(term))
    diag_ref[...] = summed / nvec


def shards(peram, elements, l1_peram, l1_elem, owners, first_ops, second_ops, product_ops, weights):
    nelem, nvec = elements.shape[:2]
    nperam, rows = peram.shape[:2]
    lanes = lax.axis_size("col")
    peers = lax.axis_size("wide")
    tasks = second_ops.shape[2]
    nproducts = product_ops.shape[2]
    diagrams = weights.shape[0]
    width = 2 * nvec
    strips = nvec // 128
    total = peers * lanes * 2
    vmem = pl.BlockSpec(memory_space=pltpu.VMEM)
    smem = pl.BlockSpec(memory_space=pltpu.SMEM)
    bf16 = jnp.bfloat16
    f32 = jnp.float32

    def kernel(*refs):
        contract(lanes, peers, *refs)

    products, sums = pl.pallas_call(
        kernel,
        out_shape=(
            jax.ShapeDtypeStruct((nproducts, lanes, 1, rows, 2, nvec), bf16),
            jax.ShapeDtypeStruct((2, diagrams), f32),
        ),
        in_specs=[vmem, pl.BlockSpec(memory_space=pl.ANY), vmem, vmem, vmem] + [smem] * 6,
        out_specs=(vmem, vmem),
        scratch_shapes=[
            pltpu.VMEM((nelem, nvec, 2, nvec), bf16),
            pltpu.VMEM((nelem, width, width), bf16),
            pltpu.VMEM((max(lanes - 1, 1), CAP_LANE, rows, 2, nvec), bf16),
            pltpu.VMEM((CAP_LANE, rows, 2, nvec), bf16),
            pltpu.VMEM((lanes, CAP_LANE, rows, 2, nvec), bf16),
            pltpu.VMEM((lanes, CAP_LANE, rows, 2, nvec), bf16),
            pltpu.VMEM((peers, lanes, rows, 2, nvec), bf16),
            pltpu.VMEM((peers, lanes, rows, 2, nvec), bf16),
            pltpu.VMEM((strips, 2 * lanes * rows, 128), f32),
            pltpu.VMEM((strips, 2 * nvec, 128), f32),
            pltpu.VMEM((lanes * rows, width), bf16),
            pltpu.VMEM((nvec, width), bf16),
            pltpu.VMEM((peers, lanes * rows, width), bf16),
            pltpu.VMEM((CAP_LANE, width, width), bf16),
            pltpu.VMEM((tasks, lanes, rows, width), bf16),
            pltpu.VMEM((tasks, lanes, rows, width), bf16),
            pltpu.VMEM((width, width), bf16),
            pltpu.VMEM((lanes * rows, nvec), f32),
            pltpu.VMEM((2, diagrams), f32),
            pltpu.VMEM((total, 2, diagrams), f32),
            pltpu.VMEM((peers, 8, 128), jnp.int32),
            pltpu.SMEM((peers, 8, 128), jnp.int32),
            pltpu.SemaphoreType.DMA((nelem,)),
            pltpu.SemaphoreType.DMA,
            pltpu.SemaphoreType.DMA((lanes, CAP_LANE)),
            pltpu.SemaphoreType.DMA((lanes, CAP_LANE)),
            pltpu.SemaphoreType.DMA((lanes,)),
            pltpu.SemaphoreType.DMA((lanes,)),
            pltpu.SemaphoreType.DMA((peers, lanes)),
            pltpu.SemaphoreType.DMA((peers, lanes)),
            pltpu.SemaphoreType.DMA((peers,)),
            pltpu.SemaphoreType.DMA((peers,)),
            pltpu.SemaphoreType.DMA((tasks,)),
            pltpu.SemaphoreType.DMA((tasks,)),
            pltpu.SemaphoreType.DMA((total,)),
            pltpu.SemaphoreType.DMA((total,)),
        ],
        compiler_params=pltpu.CompilerParams(
            collective_id=0, has_side_effects=True, vmem_limit_bytes=58 * 2**20
        ),
    )(
        peram,
        elements,
        weights.T,
        l1_elem,
        owners,
        l1_peram,
        l1_elem,
        owners,
        first_ops,
        second_ops,
        product_ops.transpose(0, 1, 3, 2),
    )
    return (products, sums.T)


def solution(mesh):
    placed = (
        P(("parts", "wide"), ("col", "pair"), None, None),
        P("parts", None, None, None),
        P(("parts", "wide"), None),
        P(("parts", "wide"), None),
        P(("parts", "wide"), None),
        P("parts", "col", None),
        P(("parts", "wide"), "col", None),
        P(("parts", "wide"), "col", None, None),
        P("parts", ("wide", "col")),
    )
    return jax.shard_map(
        shards,
        mesh=mesh,
        in_specs=placed,
        out_specs=(P(("parts", "wide", "col"), None, "pair", None, None, None), P("parts", None)),
        check_vma=False,
    )
```

```python
import math

import jax
import jax.numpy as jnp
from jax import lax
from jax.experimental import pallas as pl
from jax.experimental.pallas import tpu as pltpu
from jax.sharding import PartitionSpec as P

CAP_LANE = 3
MESH = pl.DeviceIdType.MESH


def contract(
    lanes,
    peers,
    perams_ref,
    elems_ref,
    weights_ref,
    l1_elem_vec,
    owners_vec,
    l1_peram,
    l1_elem,
    owners,
    first_ops,
    second_ops,
    product_ops,
    out_ref,
    diag_ref,
    perams_raw,
    elems_raw,
    big_elem,
    x_stage,
    own,
    arrived,
    paired,
    z_stage,
    pool,
    half_raw,
    full_raw,
    left_wide,
    right_wide,
    left_ops,
    big_right,
    q_own,
    q_other,
    big_q,
    mask,
    term,
    terms,
    ids_vec,
    ids,
    r_full,
    out_stage,
    o_sem,
    pe_sem,
    e_sem,
    ids_sem,
    x_send,
    x_recv,
    p_send,
    p_recv,
    z_send,
    z_recv,
    i_send,
    i_recv,
    q_send,
    q_recv,
    d_send,
    d_recv,
):
    here = lax.axis_index("wide")
    lane = lax.axis_index("col")
    half = lax.axis_index("pair")
    nelem = elems_ref.shape[0]
    nvec = left_wide.shape[1] // 2
    wide2 = 2 * nvec
    rows = perams_ref.shape[1]
    strips = nvec // 128
    half_rows = lanes * rows
    nblocks = owners.shape[1]
    tasks = second_ops.shape[2]
    nproducts = product_ops.shape[3]
    factor = 1.0 / math.sqrt(2.0 * nvec)
    total = peers * lanes * 2
    mine = (here * lanes + lane) * 2 + half
    bf16 = jnp.bfloat16

    def elem_copy(e):
        return pltpu.make_async_copy(elems_ref.at[e], elems_raw.at[e], e_sem.at[e])

    def out_copy(v):
        return pltpu.make_async_copy(out_stage.at[v], out_ref.at[v], o_sem.at[v])

    perams_copy = pltpu.make_async_copy(perams_ref, perams_raw, pe_sem)
    perams_copy.start()

    def coords(index):
        return {"wide": index // (lanes * 2), "col": index // 2 % lanes, "pair": index % 2}

    barrier = pltpu.get_barrier_semaphore()

    def greet(i, carry):
        other = lax.rem(mine + 1 + i, total)
        pl.semaphore_signal(barrier, inc=1, device_id=coords(other), device_id_type=MESH)
        return carry

    lax.fori_loop(0, total - 1, greet, 0)
    for e in range(nelem):
        elem_copy(e).start()

    def flat(block):
        if rows % 16 == 0:
            return block.reshape(-1, wide2)
        return block.astype(jnp.float32).reshape(-1, wide2).astype(bf16)

    def split(block):
        return block.reshape(lanes, rows, wide2)

    def expand(target, y):
        target[:nvec, :] = y
        target[nvec:, :nvec] = -y[:, nvec:]
        target[nvec:, nvec:] = y[:, :nvec]

    def strip(j, base=0):
        return slice(base + j * 128, base + (j + 1) * 128)

    def columns(raw, count):
        for j in range(strips):
            for c in range(2):
                yield c, j, raw[j, pl.ds(c, count, stride=2), :].astype(bf16)

    def gather_columns(target, raw):
        for c, j, block in columns(raw, target.shape[0]):
            target[:, strip(j, c * nvec)] = block

    def as_rows(block):
        return block.astype(jnp.float32).reshape(-1, 128)

    def blocks_of(which, owner_at):
        found = [jnp.int32(0)] * CAP_LANE
        count = jnp.int32(0)
        for b in range(nblocks):
            match = (owner_at(b) == which).astype(jnp.int32)
            for k in range(CAP_LANE):
                found[k] = jnp.where((match == 1) & (count == k), jnp.int32(b), found[k])
            count = count + match
        return found

    def x_copy(j, k):
        return pltpu.make_async_remote_copy(
            src_ref=x_stage.at[j, k],
            dst_ref=arrived.at[lane, k],
            send_sem=x_send.at[j, k],
            recv_sem=x_recv.at[j, k],
            device_id={"col": lax.rem(lane + 1 + j, lanes)},
            device_id_type=MESH,
        )

    def p_copy(j):
        q = lax.rem(lane + lanes - j, lanes)
        return pltpu.make_async_remote_copy(
            src_ref=own if j == 0 else arrived.at[q],
            dst_ref=paired.at[q],
            send_sem=p_send.at[j],
            recv_sem=p_recv.at[j],
            device_id={"pair": 1 - half},
            device_id_type=MESH,
        )

    def z_copy(i, j):
        q = lax.rem(lane + lanes - j, lanes)
        return pltpu.make_async_remote_copy(
            src_ref=z_stage.at[i, q],
            dst_ref=pool.at[here, q],
            send_sem=z_send.at[i, j],
            recv_sem=z_recv.at[i, j],
            device_id={"wide": lax.rem(here + 1 + i, peers)},
            device_id_type=MESH,
        )

    def i_copy(i):
        return pltpu.make_async_remote_copy(
            src_ref=ids_vec.at[here],
            dst_ref=ids_vec.at[here],
            send_sem=i_send.at[i],
            recv_sem=i_recv.at[i],
            device_id={"wide": lax.rem(here + 1 + i, peers)},
            device_id_type=MESH,
        )

    def q_copy(t):
        return pltpu.make_async_remote_copy(
            src_ref=q_own.at[t],
            dst_ref=q_other.at[t],
            send_sem=q_send.at[t],
            recv_sem=q_recv.at[t],
            device_id={"pair": 1 - half},
            device_id_type=MESH,
        )

    def d_copy(i):
        return pltpu.make_async_remote_copy(
            src_ref=term,
            dst_ref=terms.at[mine],
            send_sem=d_send.at[i],
            recv_sem=d_recv.at[i],
            device_id=coords(lax.rem(mine + 1 + i, total)),
            device_id_type=MESH,
        )

    def rank_for(group):
        chosen = jnp.int32(0)
        for t in range(tasks):
            entry = first_ops[group, 0, t]
            chosen = jnp.where(entry // CAP_LANE == here, entry % CAP_LANE, chosen)
        return chosen

    ids_vec[here] = jnp.zeros(ids_vec.shape[1:], jnp.int32)
    ids_vec[here, 0:1, 0:nblocks] = l1_elem_vec[...]
    ids_vec[here, 1:2, 0:nblocks] = owners_vec[...]
    picked = blocks_of(lane, lambda b: owners[0, b])
    ranks = [rank_for(lax.rem(here + 1 + i, peers)) for i in range(peers - 1)]
    rank_here = rank_for(here)
    perams_copy.wait()
    for k in range(CAP_LANE):
        own[k] = perams_raw[l1_peram[0, picked[k]]]
    pl.semaphore_wait(barrier, total - 1)
    for i in range(peers - 1):
        z_stage[i, lane] = own[ranks[i]]
        z_copy(i, 0).start()
    for j in range(lanes - 1):
        others = blocks_of(lax.rem(lane + 1 + j, lanes), lambda b: owners[0, b])
        for k in range(CAP_LANE):
            x_stage[j, k] = perams_raw[l1_peram[0, others[k]]]
            x_copy(j, k).start()
    for i in range(peers - 1):
        i_copy(i).start()
    p_copy(0).start()
    pool[here, lane] = own[rank_here]

    row_ids = lax.broadcasted_iota(jnp.int32, (rows, nvec), 0)
    col_ids = lax.broadcasted_iota(jnp.int32, (rows, nvec), 1)
    for q in range(lanes):
        mask[q * rows : (q + 1) * rows, :] = (
            col_ids == row_ids + (2 * q + half) * rows
        ).astype(jnp.float32)

    def convert_elem(e):
        elem_copy(e).wait()
        for j in range(strips):
            full_raw[j] = as_rows(elems_raw[e, :, :, strip(j)])
        for c, j, block in columns(full_raw, nvec):
            low, high = j * 128, (j + 1) * 128
            if c == 0:
                big_elem[e, :nvec, low:high] = block
                big_elem[e, nvec:, nvec + low : nvec + high] = block
            else:
                big_elem[e, :nvec, nvec + low : nvec + high] = block
                big_elem[e, nvec:, low:high] = -block

    convert_elem(0)
    for j in range(lanes - 1):
        for k in range(CAP_LANE):
            x_copy(j, k).wait_recv()
    for j in range(1, lanes):
        q = lax.rem(lane + lanes - j, lanes)
        for i in range(peers - 1):
            z_stage[i, q] = arrived[q, ranks[i]]
            z_copy(i, j).start()
        p_copy(j).start()
        pool[here, q] = arrived[q, rank_here]
    for e in range(1, nelem):
        convert_elem(e)
    for i in range(peers - 1):
        i_copy(i).wait()
    ids_copy = pltpu.make_async_copy(ids_vec, ids, ids_sem)
    ids_copy.start()
    ids_copy.wait()
    for j in range(lanes):
        p_copy(j).wait_recv()

    for k in range(CAP_LANE):
        for n in range(lanes):
            q = lax.rem(lane + lanes - n, lanes)
            for side in range(2):
                at = half if side == 0 else 1 - half
                start = pl.multiple_of((2 * q + at) * (2 * rows), 8)
                for j in range(strips):
                    if side == 1:
                        block = paired[q, k, :, :, strip(j)]
                    elif n == 0:
                        block = own[k, :, :, strip(j)]
                    else:
                        block = arrived[q, k, :, :, strip(j)]
                    full_raw[j, pl.ds(start, 2 * rows), :] = as_rows(block)
        gather_columns(right_wide, full_raw)
        block = jnp.dot(
            right_wide[...],
            big_elem[l1_elem[0, picked[k]]],
            preferred_element_type=jnp.float32,
        )
        expand(big_right.at[k], block.astype(bf16))

    def source_element(source):
        wanted = jnp.int32(0)
        for t in range(tasks):
            entry = first_ops[here, 0, t]
            wanted = jnp.where(entry // CAP_LANE == source, entry % CAP_LANE, wanted)
        found = blocks_of(lane, lambda b: ids[source, 1, b])
        chosen = found[0]
        for k in range(1, CAP_LANE):
            chosen = jnp.where(wanted == k, found[k], chosen)
        return ids[source, 0, chosen]

    def make_left(source):
        for j in range(strips):
            half_raw[j] = as_rows(pool[source, :, :, :, strip(j)])
        gather_columns(left_wide, half_raw)
        left_ops[source] = jnp.dot(
            left_wide[...],
            big_elem[source_element(source)],
            preferred_element_type=jnp.float32,
        ).astype(bf16)

    make_left(here)

    def one_source(i, carry):
        for j in range(lanes):
            z_copy(i, j).wait_recv()
        make_left(lax.rem(here + peers - 1 - i, peers))
        return carry

    lax.fori_loop(0, peers - 1, one_source, 0)

    def one_task(t, carry):
        left = left_ops[first_ops[here, 0, t] // CAP_LANE]
        full = jnp.dot(left, big_right[second_ops[0, 0, t]], preferred_element_type=jnp.float32)
        q_own[t] = split(full * factor).astype(bf16)
        q_copy(t).start()
        return carry

    lax.fori_loop(0, tasks, one_task, 0)

    for j in range(lanes - 1):
        for k in range(CAP_LANE):
            x_copy(j, k).wait_send()
    for j in range(lanes):
        p_copy(j).wait_send()
        for i in range(peers - 1):
            z_copy(i, j).wait_send()

    def q_done(t, carry):
        q_copy(t).wait()
        return carry

    lax.fori_loop(0, tasks, q_done, 0)

    def both_halves(target, mine_half, other_half):
        pieces = []
        for q in range(lanes):
            a = mine_half(q).astype(jnp.float32)
            b = other_half(q).astype(jnp.float32)
            pieces.append(jnp.where(half == 0, a, b))
            pieces.append(jnp.where(half == 0, b, a))
        expand(target, jnp.concatenate(pieces, axis=0).astype(bf16))

    sums = [jnp.zeros((1, term.shape[1]), jnp.float32)] * 2
    for v in range(nproducts):
        left_id = product_ops[0, 0, 0, v]
        right_id = product_ops[0, 0, 1, v]
        both_halves(big_q, lambda q: q_own[right_id, q], lambda q: q_other[right_id, q])
        full = jnp.dot(flat(q_own[left_id]), big_q[...], preferred_element_type=jnp.float32) * factor
        weight = weights_ref[v : v + 1, :].astype(jnp.float32)
        r_full[v] = full
        for c in range(2):
            picked_diag = jnp.sum(
                full[:, c * nvec : (c + 1) * nvec] * mask[...], axis=0, keepdims=True
            )
            sums[c] = sums[c] + weight * jnp.sum(picked_diag, axis=1, keepdims=True)

    for c in range(2):
        term[c : c + 1, :] = sums[c]
    terms[mine] = term[...]

    def d_start(i, carry):
        d_copy(i).start()
        return carry

    def d_done(i, carry):
        d_copy(i).wait()
        return carry

    lax.fori_loop(0, total - 1, d_start, 0)
    for v in range(nproducts):
        for j in range(strips):
            for c in range(2):
                half_raw[j, pl.ds(c, half_rows, stride=2), :] = r_full[v, :, strip(j, c * nvec)]
            out_stage[v, :, 0, :, :, strip(j)] = (
                half_raw[j].astype(bf16).reshape(lanes, rows, 2, 128)
            )
        out_copy(v).start()
    lax.fori_loop(0, total - 1, d_done, 0)
    summed = lax.fori_loop(0, total, lambda i, acc: acc + terms[i], jnp.zeros_like(term))
    diag_ref[...] = summed / nvec
    for v in range(nproducts):
        out_copy(v).wait()


def relay(source, target, sems):
    copies = [
        pltpu.make_async_copy(source.at[v], target.at[v], sems.at[v])
        for v in range(source.shape[0])
    ]
    for copy in copies:
        copy.start()
    for copy in copies:
        copy.wait()


def shards(peram, elements, l1_peram, l1_elem, owners, first_ops, second_ops, product_ops, weights):
    nelem, nvec = elements.shape[:2]
    nperam, rows = peram.shape[:2]
    lanes = lax.axis_size("col")
    peers = lax.axis_size("wide")
    tasks = second_ops.shape[2]
    nproducts = product_ops.shape[2]
    diagrams = weights.shape[0]
    width = 2 * nvec
    strips = nvec // 128
    total = peers * lanes * 2
    vmem = pl.BlockSpec(memory_space=pltpu.VMEM)
    smem = pl.BlockSpec(memory_space=pltpu.SMEM)
    anywhere = pl.BlockSpec(memory_space=pl.ANY)
    bf16 = jnp.bfloat16
    f32 = jnp.float32

    def kernel(*refs):
        contract(lanes, peers, *refs)

    products, sums = pl.pallas_call(
        kernel,
        out_shape=(
            jax.ShapeDtypeStruct((nproducts, lanes, 1, rows, 2, nvec), bf16),
            jax.ShapeDtypeStruct((2, diagrams), f32),
        ),
        in_specs=[anywhere] * 2 + [vmem] * 3 + [smem] * 6,
        out_specs=(anywhere, vmem),
        scratch_shapes=[
            pltpu.VMEM((nperam, rows, 2, nvec), bf16),
            pltpu.VMEM((nelem, nvec, 2, nvec), bf16),
            pltpu.VMEM((nelem, width, width), bf16),
            pltpu.VMEM((max(lanes - 1, 1), CAP_LANE, rows, 2, nvec), bf16),
            pltpu.VMEM((CAP_LANE, rows, 2, nvec), bf16),
            pltpu.VMEM((lanes, CAP_LANE, rows, 2, nvec), bf16),
            pltpu.VMEM((lanes, CAP_LANE, rows, 2, nvec), bf16),
            pltpu.VMEM((peers, lanes, rows, 2, nvec), bf16),
            pltpu.VMEM((peers, lanes, rows, 2, nvec), bf16),
            pltpu.VMEM((strips, 2 * lanes * rows, 128), f32),
            pltpu.VMEM((strips, 2 * nvec, 128), f32),
            pltpu.VMEM((lanes * rows, width), bf16),
            pltpu.VMEM((nvec, width), bf16),
            pltpu.VMEM((peers, lanes * rows, width), bf16),
            pltpu.VMEM((CAP_LANE, width, width), bf16),
            pltpu.VMEM((tasks, lanes, rows, width), bf16),
            pltpu.VMEM((tasks, lanes, rows, width), bf16),
            pltpu.VMEM((width, width), bf16),
            pltpu.VMEM((lanes * rows, nvec), f32),
            pltpu.VMEM((2, diagrams), f32),
            pltpu.VMEM((total, 2, diagrams), f32),
            pltpu.VMEM((peers, 8, 128), jnp.int32),
            pltpu.SMEM((peers, 8, 128), jnp.int32),
            pltpu.VMEM((nproducts, lanes * rows, width), f32),
            pltpu.VMEM((nproducts, lanes, 1, rows, 2, nvec), bf16),
            pltpu.SemaphoreType.DMA((nproducts,)),
            pltpu.SemaphoreType.DMA,
            pltpu.SemaphoreType.DMA((nelem,)),
            pltpu.SemaphoreType.DMA,
            pltpu.SemaphoreType.DMA((lanes, CAP_LANE)),
            pltpu.SemaphoreType.DMA((lanes, CAP_LANE)),
            pltpu.SemaphoreType.DMA((lanes,)),
            pltpu.SemaphoreType.DMA((lanes,)),
            pltpu.SemaphoreType.DMA((peers, lanes)),
            pltpu.SemaphoreType.DMA((peers, lanes)),
            pltpu.SemaphoreType.DMA((peers,)),
            pltpu.SemaphoreType.DMA((peers,)),
            pltpu.SemaphoreType.DMA((tasks,)),
            pltpu.SemaphoreType.DMA((tasks,)),
            pltpu.SemaphoreType.DMA((total,)),
            pltpu.SemaphoreType.DMA((total,)),
        ],
        compiler_params=pltpu.CompilerParams(
            collective_id=0, has_side_effects=True, vmem_limit_bytes=58 * 2**20
        ),
    )(
        peram,
        elements,
        weights.T,
        l1_elem,
        owners,
        l1_peram,
        l1_elem,
        owners,
        first_ops,
        second_ops,
        product_ops.transpose(0, 1, 3, 2),
    )
    products = pl.pallas_call(
        relay,
        out_shape=jax.ShapeDtypeStruct(products.shape, bf16),
        in_specs=[anywhere],
        out_specs=anywhere,
        scratch_shapes=[pltpu.SemaphoreType.DMA((nproducts,))],
    )(products)
    return (products, sums.T)


def solution(mesh):
    placed = (
        P(("parts", "wide"), ("col", "pair"), None, None),
        P("parts", None, None, None),
        P(("parts", "wide"), None),
        P(("parts", "wide"), None),
        P(("parts", "wide"), None),
        P("parts", "col", None),
        P(("parts", "wide"), "col", None),
        P(("parts", "wide"), "col", None, None),
        P("parts", ("wide", "col")),
    )
    return jax.shard_map(
        shards,
        mesh=mesh,
        in_specs=placed,
        out_specs=(P(("parts", "wide", "col"), None, "pair", None, None, None), P("parts", None)),
        check_vma=False,
    )
```

```python
import math

import jax
import jax.numpy as jnp
from jax import lax
from jax.experimental import pallas as pl
from jax.experimental.pallas import tpu as pltpu
from jax.sharding import PartitionSpec as P

CAP_LANE = 3
MESH = pl.DeviceIdType.MESH


def contract(
    lanes,
    peers,
    perams_ref,
    elems_ref,
    weights_ref,
    l1_elem_vec,
    owners_vec,
    l1_peram,
    l1_elem,
    owners,
    first_ops,
    second_ops,
    product_ops,
    out_ref,
    diag_ref,
    perams_raw,
    elems_raw,
    big_elem,
    x_stage,
    own,
    arrived,
    paired,
    z_stage,
    pool,
    half_raw,
    full_raw,
    left_wide,
    right_wide,
    left_ops,
    big_right,
    q_own,
    q_other,
    big_q,
    mask,
    term,
    terms,
    ids_vec,
    ids,
    r_full,
    out_stage,
    o_sem,
    pe_sem,
    e_sem,
    ids_sem,
    x_send,
    x_recv,
    p_send,
    p_recv,
    z_send,
    z_recv,
    i_send,
    i_recv,
    q_send,
    q_recv,
    d_send,
    d_recv,
):
    here = lax.axis_index("wide")
    lane = lax.axis_index("col")
    half = lax.axis_index("pair")
    nelem = elems_ref.shape[0]
    nvec = left_wide.shape[1] // 2
    wide2 = 2 * nvec
    rows = perams_ref.shape[1]
    strips = nvec // 128
    half_rows = lanes * rows
    nblocks = owners.shape[1]
    tasks = second_ops.shape[2]
    nproducts = product_ops.shape[3]
    factor = 1.0 / math.sqrt(2.0 * nvec)
    total = peers * lanes * 2
    mine = (here * lanes + lane) * 2 + half
    bf16 = jnp.bfloat16

    def elem_copy(e):
        return pltpu.make_async_copy(elems_ref.at[e], elems_raw.at[e], e_sem.at[e])

    def out_copy(v):
        return pltpu.make_async_copy(out_stage.at[v], out_ref.at[v], o_sem.at[v])

    perams_copy = pltpu.make_async_copy(perams_ref, perams_raw, pe_sem)
    perams_copy.start()

    def coords(index):
        return {"wide": index // (lanes * 2), "col": index // 2 % lanes, "pair": index % 2}

    barrier = pltpu.get_barrier_semaphore()

    def greet(i, carry):
        other = lax.rem(mine + 1 + i, total)
        pl.semaphore_signal(barrier, inc=1, device_id=coords(other), device_id_type=MESH)
        return carry

    lax.fori_loop(0, total - 1, greet, 0)
    for e in range(nelem):
        elem_copy(e).start()

    def flat(block):
        if rows % 16 == 0:
            return block.reshape(-1, wide2)
        return block.astype(jnp.float32).reshape(-1, wide2).astype(bf16)

    def split(block):
        return block.reshape(lanes, rows, wide2)

    def expand(target, y):
        target[:nvec, :] = y
        target[nvec:, :nvec] = -y[:, nvec:]
        target[nvec:, nvec:] = y[:, :nvec]

    def strip(j, base=0):
        return slice(base + j * 128, base + (j + 1) * 128)

    def columns(raw, count):
        for j in range(strips):
            for c in range(2):
                yield c, j, raw[j, pl.ds(c, count, stride=2), :].astype(bf16)

    def gather_columns(target, raw):
        for c, j, block in columns(raw, target.shape[0]):
            target[:, strip(j, c * nvec)] = block

    def as_rows(block):
        return block.astype(jnp.float32).reshape(-1, 128)

    def blocks_of(which, owner_at):
        found = [jnp.int32(0)] * CAP_LANE
        count = jnp.int32(0)
        for b in range(nblocks):
            match = (owner_at(b) == which).astype(jnp.int32)
            for k in range(CAP_LANE):
                found[k] = jnp.where((match == 1) & (count == k), jnp.int32(b), found[k])
            count = count + match
        return found

    def x_copy(j, k):
        return pltpu.make_async_remote_copy(
            src_ref=x_stage.at[j, k],
            dst_ref=arrived.at[lane, k],
            send_sem=x_send.at[j, k],
            recv_sem=x_recv.at[j, k],
            device_id={"col": lax.rem(lane + 1 + j, lanes)},
            device_id_type=MESH,
        )

    def p_copy(j):
        q = lax.rem(lane + lanes - j, lanes)
        return pltpu.make_async_remote_copy(
            src_ref=own if j == 0 else arrived.at[q],
            dst_ref=paired.at[q],
            send_sem=p_send.at[j],
            recv_sem=p_recv.at[j],
            device_id={"pair": 1 - half},
            device_id_type=MESH,
        )

    def z_copy(i, j):
        q = lax.rem(lane + lanes - j, lanes)
        return pltpu.make_async_remote_copy(
            src_ref=z_stage.at[i, q],
            dst_ref=pool.at[here, q],
            send_sem=z_send.at[i, j],
            recv_sem=z_recv.at[i, j],
            device_id={"wide": lax.rem(here + 1 + i, peers)},
            device_id_type=MESH,
        )

    def i_copy(i):
        return pltpu.make_async_remote_copy(
            src_ref=ids_vec.at[here],
            dst_ref=ids_vec.at[here],
            send_sem=i_send.at[i],
            recv_sem=i_recv.at[i],
            device_id={"wide": lax.rem(here + 1 + i, peers)},
            device_id_type=MESH,
        )

    def q_copy(t):
        return pltpu.make_async_remote_copy(
            src_ref=q_own.at[t],
            dst_ref=q_other.at[t],
            send_sem=q_send.at[t],
            recv_sem=q_recv.at[t],
            device_id={"pair": 1 - half},
            device_id_type=MESH,
        )

    def d_copy(i):
        return pltpu.make_async_remote_copy(
            src_ref=term,
            dst_ref=terms.at[mine],
            send_sem=d_send.at[i],
            recv_sem=d_recv.at[i],
            device_id=coords(lax.rem(mine + 1 + i, total)),
            device_id_type=MESH,
        )

    def rank_for(group):
        chosen = jnp.int32(0)
        for t in range(tasks):
            entry = first_ops[group, 0, t]
            chosen = jnp.where(entry // CAP_LANE == here, entry % CAP_LANE, chosen)
        return chosen

    ids_vec[here] = jnp.zeros(ids_vec.shape[1:], jnp.int32)
    ids_vec[here, 0:1, 0:nblocks] = l1_elem_vec[...]
    ids_vec[here, 1:2, 0:nblocks] = owners_vec[...]
    picked = blocks_of(lane, lambda b: owners[0, b])
    ranks = [rank_for(lax.rem(here + 1 + i, peers)) for i in range(peers - 1)]
    rank_here = rank_for(here)
    perams_copy.wait()
    for k in range(CAP_LANE):
        own[k] = perams_raw[l1_peram[0, picked[k]]]
    pl.semaphore_wait(barrier, total - 1)
    for i in range(peers - 1):
        z_stage[i, lane] = own[ranks[i]]
        z_copy(i, 0).start()
    for j in range(lanes - 1):
        others = blocks_of(lax.rem(lane + 1 + j, lanes), lambda b: owners[0, b])
        for k in range(CAP_LANE):
            x_stage[j, k] = perams_raw[l1_peram[0, others[k]]]
            x_copy(j, k).start()
    for i in range(peers - 1):
        i_copy(i).start()
    p_copy(0).start()
    pool[here, lane] = own[rank_here]

    row_ids = lax.broadcasted_iota(jnp.int32, (rows, nvec), 0)
    col_ids = lax.broadcasted_iota(jnp.int32, (rows, nvec), 1)
    for q in range(lanes):
        mask[q * rows : (q + 1) * rows, :] = (
            col_ids == row_ids + (2 * q + half) * rows
        ).astype(jnp.float32)

    def convert_elem(e):
        elem_copy(e).wait()
        for j in range(strips):
            full_raw[j] = as_rows(elems_raw[e, :, :, strip(j)])
        for c, j, block in columns(full_raw, nvec):
            low, high = j * 128, (j + 1) * 128
            if c == 0:
                big_elem[e, :nvec, low:high] = block
                big_elem[e, nvec:, nvec + low : nvec + high] = block
            else:
                big_elem[e, :nvec, nvec + low : nvec + high] = block
                big_elem[e, nvec:, low:high] = -block

    convert_elem(0)
    for j in range(lanes - 1):
        for k in range(CAP_LANE):
            x_copy(j, k).wait_recv()
    for j in range(1, lanes):
        q = lax.rem(lane + lanes - j, lanes)
        for i in range(peers - 1):
            z_stage[i, q] = arrived[q, ranks[i]]
            z_copy(i, j).start()
        p_copy(j).start()
        pool[here, q] = arrived[q, rank_here]
    for e in range(1, nelem):
        convert_elem(e)
    for i in range(peers - 1):
        i_copy(i).wait()
    ids_copy = pltpu.make_async_copy(ids_vec, ids, ids_sem)
    ids_copy.start()
    ids_copy.wait()
    for j in range(lanes):
        p_copy(j).wait_recv()

    for k in range(CAP_LANE):
        for n in range(lanes):
            q = lax.rem(lane + lanes - n, lanes)
            for side in range(2):
                at = half if side == 0 else 1 - half
                start = pl.multiple_of((2 * q + at) * (2 * rows), 8)
                for j in range(strips):
                    if side == 1:
                        block = paired[q, k, :, :, strip(j)]
                    elif n == 0:
                        block = own[k, :, :, strip(j)]
                    else:
                        block = arrived[q, k, :, :, strip(j)]
                    full_raw[j, pl.ds(start, 2 * rows), :] = as_rows(block)
        gather_columns(right_wide, full_raw)
        block = jnp.dot(
            right_wide[...],
            big_elem[l1_elem[0, picked[k]]],
            preferred_element_type=jnp.float32,
        )
        expand(big_right.at[k], block.astype(bf16))

    def source_element(source):
        wanted = jnp.int32(0)
        for t in range(tasks):
            entry = first_ops[here, 0, t]
            wanted = jnp.where(entry // CAP_LANE == source, entry % CAP_LANE, wanted)
        found = blocks_of(lane, lambda b: ids[source, 1, b])
        chosen = found[0]
        for k in range(1, CAP_LANE):
            chosen = jnp.where(wanted == k, found[k], chosen)
        return ids[source, 0, chosen]

    def make_left(source):
        for j in range(strips):
            half_raw[j] = as_rows(pool[source, :, :, :, strip(j)])
        gather_columns(left_wide, half_raw)
        left_ops[source] = jnp.dot(
            left_wide[...],
            big_elem[source_element(source)],
            preferred_element_type=jnp.float32,
        ).astype(bf16)

    make_left(here)

    def one_source(i, carry):
        for j in range(lanes):
            z_copy(i, j).wait_recv()
        make_left(lax.rem(here + peers - 1 - i, peers))
        return carry

    lax.fori_loop(0, peers - 1, one_source, 0)

    def one_task(t, carry):
        left = left_ops[first_ops[here, 0, t] // CAP_LANE]
        full = jnp.dot(left, big_right[second_ops[0, 0, t]], preferred_element_type=jnp.float32)
        q_own[t] = split(full * factor).astype(bf16)
        q_copy(t).start()
        return carry

    lax.fori_loop(0, tasks, one_task, 0)

    for j in range(lanes - 1):
        for k in range(CAP_LANE):
            x_copy(j, k).wait_send()
    for j in range(lanes):
        p_copy(j).wait_send()
        for i in range(peers - 1):
            z_copy(i, j).wait_send()

    def q_done(t, carry):
        q_copy(t).wait()
        return carry

    lax.fori_loop(0, tasks, q_done, 0)

    def both_halves(target, mine_half, other_half):
        pieces = []
        for q in range(lanes):
            a = mine_half(q).astype(jnp.float32)
            b = other_half(q).astype(jnp.float32)
            pieces.append(jnp.where(half == 0, a, b))
            pieces.append(jnp.where(half == 0, b, a))
        expand(target, jnp.concatenate(pieces, axis=0).astype(bf16))

    sums = [jnp.zeros((1, term.shape[1]), jnp.float32)] * 2
    for v in range(nproducts):
        left_id = product_ops[0, 0, 0, v]
        right_id = product_ops[0, 0, 1, v]
        both_halves(big_q, lambda q: q_own[right_id, q], lambda q: q_other[right_id, q])
        full = jnp.dot(flat(q_own[left_id]), big_q[...], preferred_element_type=jnp.float32) * factor
        weight = weights_ref[v : v + 1, :].astype(jnp.float32)
        r_full[v] = full
        for c in range(2):
            picked_diag = jnp.sum(
                full[:, c * nvec : (c + 1) * nvec] * mask[...], axis=0, keepdims=True
            )
            sums[c] = sums[c] + weight * jnp.sum(picked_diag, axis=1, keepdims=True)

    for c in range(2):
        term[c : c + 1, :] = sums[c]
    terms[mine] = term[...]

    def d_start(i, carry):
        d_copy(i).start()
        return carry

    def d_done(i, carry):
        d_copy(i).wait()
        return carry

    lax.fori_loop(0, total - 1, d_start, 0)
    for v in range(nproducts):
        for j in range(strips):
            for c in range(2):
                half_raw[j, pl.ds(c, half_rows, stride=2), :] = r_full[v, :, strip(j, c * nvec)]
            out_stage[v, :, 0, :, :, strip(j)] = (
                half_raw[j].astype(bf16).reshape(lanes, rows, 2, 128)
            )
        out_copy(v).start()
    lax.fori_loop(0, total - 1, d_done, 0)
    summed = lax.fori_loop(0, total, lambda i, acc: acc + terms[i], jnp.zeros_like(term))
    diag_ref[...] = summed / nvec
    for v in range(nproducts):
        out_copy(v).wait()


def relay(source, target, sems):
    copies = [
        pltpu.make_async_copy(source.at[v], target.at[v], sems.at[v])
        for v in range(source.shape[0])
    ]
    for copy in copies:
        copy.start()
    for copy in copies:
        copy.wait()


def shards(peram, elements, l1_peram, l1_elem, owners, first_ops, second_ops, product_ops, weights):
    nelem, nvec = elements.shape[:2]
    nperam, rows = peram.shape[:2]
    lanes = lax.axis_size("col")
    peers = lax.axis_size("wide")
    tasks = second_ops.shape[2]
    nproducts = product_ops.shape[2]
    diagrams = weights.shape[0]
    width = 2 * nvec
    strips = nvec // 128
    total = peers * lanes * 2
    vmem = pl.BlockSpec(memory_space=pltpu.VMEM)
    smem = pl.BlockSpec(memory_space=pltpu.SMEM)
    anywhere = pl.BlockSpec(memory_space=pl.ANY)
    bf16 = jnp.bfloat16
    f32 = jnp.float32

    def kernel(*refs):
        contract(lanes, peers, *refs)

    products, sums = pl.pallas_call(
        kernel,
        out_shape=(
            jax.ShapeDtypeStruct((nproducts, lanes, 1, rows, 2, nvec), bf16),
            jax.ShapeDtypeStruct((2, diagrams), f32),
        ),
        in_specs=[anywhere] * 2 + [vmem] * 3 + [smem] * 6,
        out_specs=(anywhere, vmem),
        scratch_shapes=[
            pltpu.VMEM((nperam, rows, 2, nvec), bf16),
            pltpu.VMEM((nelem, nvec, 2, nvec), bf16),
            pltpu.VMEM((nelem, width, width), bf16),
            pltpu.VMEM((max(lanes - 1, 1), CAP_LANE, rows, 2, nvec), bf16),
            pltpu.VMEM((CAP_LANE, rows, 2, nvec), bf16),
            pltpu.VMEM((lanes, CAP_LANE, rows, 2, nvec), bf16),
            pltpu.VMEM((lanes, CAP_LANE, rows, 2, nvec), bf16),
            pltpu.VMEM((peers, lanes, rows, 2, nvec), bf16),
            pltpu.VMEM((peers, lanes, rows, 2, nvec), bf16),
            pltpu.VMEM((strips, 2 * lanes * rows, 128), f32),
            pltpu.VMEM((strips, 2 * nvec, 128), f32),
            pltpu.VMEM((lanes * rows, width), bf16),
            pltpu.VMEM((nvec, width), bf16),
            pltpu.VMEM((peers, lanes * rows, width), bf16),
            pltpu.VMEM((CAP_LANE, width, width), bf16),
            pltpu.VMEM((tasks, lanes, rows, width), bf16),
            pltpu.VMEM((tasks, lanes, rows, width), bf16),
            pltpu.VMEM((width, width), bf16),
            pltpu.VMEM((lanes * rows, nvec), f32),
            pltpu.VMEM((2, diagrams), f32),
            pltpu.VMEM((total, 2, diagrams), f32),
            pltpu.VMEM((peers, 8, 128), jnp.int32),
            pltpu.SMEM((peers, 8, 128), jnp.int32),
            pltpu.VMEM((nproducts, lanes * rows, width), f32),
            pltpu.VMEM((nproducts, lanes, 1, rows, 2, nvec), bf16),
            pltpu.SemaphoreType.DMA((nproducts,)),
            pltpu.SemaphoreType.DMA,
            pltpu.SemaphoreType.DMA((nelem,)),
            pltpu.SemaphoreType.DMA,
            pltpu.SemaphoreType.DMA((lanes, CAP_LANE)),
            pltpu.SemaphoreType.DMA((lanes, CAP_LANE)),
            pltpu.SemaphoreType.DMA((lanes,)),
            pltpu.SemaphoreType.DMA((lanes,)),
            pltpu.SemaphoreType.DMA((peers, lanes)),
            pltpu.SemaphoreType.DMA((peers, lanes)),
            pltpu.SemaphoreType.DMA((peers,)),
            pltpu.SemaphoreType.DMA((peers,)),
            pltpu.SemaphoreType.DMA((tasks,)),
            pltpu.SemaphoreType.DMA((tasks,)),
            pltpu.SemaphoreType.DMA((total,)),
            pltpu.SemaphoreType.DMA((total,)),
        ],
        compiler_params=pltpu.CompilerParams(
            collective_id=0, has_side_effects=True, vmem_limit_bytes=58 * 2**20
        ),
    )(
        peram,
        elements,
        weights.T,
        l1_elem,
        owners,
        l1_peram,
        l1_elem,
        owners,
        first_ops,
        second_ops,
        product_ops.transpose(0, 1, 3, 2),
    )
    products = pl.pallas_call(
        relay,
        out_shape=jax.ShapeDtypeStruct(products.shape, bf16),
        in_specs=[vmem],
        out_specs=anywhere,
        scratch_shapes=[pltpu.SemaphoreType.DMA((nproducts,))],
        compiler_params=pltpu.CompilerParams(vmem_limit_bytes=58 * 2**20),
    )(products)
    return (products, sums.T)


def solution(mesh):
    placed = (
        P(("parts", "wide"), ("col", "pair"), None, None),
        P("parts", None, None, None),
        P(("parts", "wide"), None),
        P(("parts", "wide"), None),
        P(("parts", "wide"), None),
        P("parts", "col", None),
        P(("parts", "wide"), "col", None),
        P(("parts", "wide"), "col", None, None),
        P("parts", ("wide", "col")),
    )
    return jax.shard_map(
        shards,
        mesh=mesh,
        in_specs=placed,
        out_specs=(P(("parts", "wide", "col"), None, "pair", None, None, None), P("parts", None)),
        check_vma=False,
    )
```
